256 devices in a mesh: dp: 16 (over z, x_lo), ctx: 16 (over x_hi, y, core).
Axes of the slice: x: 4 (x_hi: 2, x_lo: 2; x = x_hi * 2 + x_lo), y: 4, z: 8, core: 2. Of those that a mesh axis runs over, the one named last changes fastest.
Arguments:
- hidden: bfloat16 [16, 2048, 4096], P('dp', 'ctx'), may hold values from -6 to 6
- queries: bfloat16 [16, 2048, 4096], P('dp', 'ctx'), may hold values from -5 to 5
- keys: bfloat16 [16, 2048, 512], P('dp', 'ctx'), may hold values from -5 to 5
- values: bfloat16 [16, 2048, 512], P('dp', 'ctx'), may hold values from -8 to 8
- upstream: bfloat16 [16, 2048, 4096], P('dp', 'ctx'), may hold values from -0.19824219 to 0.19824219
Outputs:
- attended: bfloat16 [16, 2048, 4096], P('dp', 'ctx')
- kv_grads: float32 [4096, 1024], P(('dp', 'ctx'))
The draws below stay inside these ranges and needn't reach their ends.
All inputs are finite; a program needn't handle non-finite values.
Results may differ from the reference program's by a relative error of at most 0.015.
Values may be sent and summed in bfloat16 or wider, within the bound.
A program may use at most 128 MiB of HBM per device.

```python
import jax
import jax.numpy as jnp
from jax import lax

D = 4096
H = 32
KV = 4
HD = 128
LENGTH = 2048
BATCH = 16
TOKENS = 32768


def draw_queries(key, part):
    key = jax.random.fold_in(key, 3)
    base = jnp.clip(jax.random.normal(key, (BATCH, LENGTH, H * HD), jnp.float32), -4.0, 4.0)
    return base.astype(jnp.bfloat16)


def draw_keys(key, part):
    key = jax.random.fold_in(key, 5)
    base = jnp.clip(jax.random.normal(key, (BATCH, LENGTH, KV * HD), jnp.float32), -4.0, 4.0)
    return base.astype(jnp.bfloat16)


def block_scale(key, shape, shards, smallest, high):
    loudness = 1.0
    for dim, blocks in shards:
        draws = jax.random.uniform(jax.random.fold_in(jax.random.fold_in(key, 6), dim), (blocks,), jnp.float32, smallest / len(shards), high / len(shards))
        loudness = loudness * jnp.repeat(jnp.exp(draws), shape[dim] // blocks).reshape((-1,) + (1,) * (len(shape) - 1 - dim))
    return loudness


def gaussian(stream_key, shape, deviation, most, split=(), kind=jnp.bfloat16):
    factor_of = block_scale(stream_key, shape, split, -0.22, 0.18) if split else 1.0
    drawn = jax.random.normal(stream_key, shape, jnp.float32) * deviation * factor_of
    return jnp.minimum(jnp.maximum(drawn, -most), most).astype(kind)


def setup_inputs(seed: int = 0) -> dict:
    key_list = jax.random.split(jax.random.key(seed), 6)
    return {
        "hidden": gaussian(key_list[0], (BATCH, LENGTH, D), 1.0, 6.0, ((0, 16), (1, 16))),
        "queries": draw_queries(jax.random.fold_in(key_list[5], 71), 0),
        "keys": draw_keys(jax.random.fold_in(key_list[5], 71), 0),
        "values": gaussian(key_list[3], (BATCH, LENGTH, KV * HD), 2.0, 8.0, ((0, 16), (1, 16))),
        "upstream": gaussian(key_list[4], (BATCH, LENGTH, H * HD), (6 * TOKENS ** -0.5), 0.19824219, ((0, 16), (1, 16))),
    }


def attend(query_seq, key_seq, value_seq, grad_seq, kv_local, group_size):
    length = query_seq.shape[0]
    inv_root = HD ** -0.5
    block_rows = 512 if length % 512 == 0 else length
    keys3 = key_seq.astype(jnp.float32).reshape(length, kv_local, HD)
    vals3 = value_seq.astype(jnp.float32).reshape(length, kv_local, HD)
    positions = jnp.arange(length)

    def block_step(running, first_row):
        key_acc, val_acc = running
        query_block = lax.dynamic_slice_in_dim(query_seq, first_row, block_rows, 0).astype(jnp.float32)
        query_block = query_block.reshape(block_rows, kv_local, group_size, HD)
        grad_block = lax.dynamic_slice_in_dim(grad_seq, first_row, block_rows, 0).astype(jnp.float32)
        grad_block = grad_block.reshape(block_rows, kv_local, group_size, HD)
        scores = jnp.einsum("qgrd,kgd->grqk", query_block, keys3) * inv_root
        rows_at = first_row + jnp.arange(block_rows)
        allowed = positions[None, :] <= rows_at[:, None]
        scores = jnp.where(allowed, scores, -jnp.inf)
        chances = jnp.exp(scores - jnp.max(scores, axis=-1, keepdims=True))
        chances = chances / jnp.sum(chances, axis=-1, keepdims=True)
        shares = chances.astype(jnp.bfloat16).astype(jnp.float32)
        attended = jnp.einsum("grqk,kgd->qgrd", shares, vals3).astype(jnp.bfloat16)
        dshares = jnp.einsum("qgrd,kgd->grqk", grad_block, vals3)
        inner_sum = jnp.sum(chances * dshares, axis=-1, keepdims=True)
        dscores = (chances * (dshares - inner_sum) * inv_root).astype(jnp.bfloat16).astype(jnp.float32)
        key_acc = key_acc + jnp.einsum("grqk,qgrd->kgrd", dscores, query_block)
        val_acc = val_acc + jnp.einsum("grqk,qgrd->kgrd", shares, grad_block)
        return (key_acc, val_acc), attended.reshape(block_rows, kv_local * group_size * HD)

    empty_acc = jnp.zeros((length, kv_local, group_size, HD), jnp.float32)
    starts = jnp.arange(length // block_rows, dtype=jnp.int32) * block_rows
    (key_acc, val_acc), blocks = lax.scan(block_step, (empty_acc, empty_acc), starts)
    attended = blocks.reshape(length, kv_local * group_size * HD)
    key_terms = key_acc.astype(jnp.bfloat16).reshape(length, kv_local * group_size * HD)
    value_terms = val_acc.astype(jnp.bfloat16).reshape(length, kv_local * group_size * HD)
    return attended, key_terms, value_terms


def sequence_terms(pieces):
    hidden_seq, query_seq, key_seq, value_seq, grad_seq = pieces
    length = query_seq.shape[0]
    attended, key_terms, value_terms = attend(query_seq, key_seq, value_seq, grad_seq, KV, H // KV)
    key_grads = key_terms.astype(jnp.float32).reshape(length, KV, H // KV, HD).sum(axis=2)
    key_grads = key_grads.astype(jnp.bfloat16).reshape(length, KV * HD)
    value_grads = value_terms.astype(jnp.float32).reshape(length, KV, H // KV, HD).sum(axis=2)
    value_grads = value_grads.astype(jnp.bfloat16).reshape(length, KV * HD)
    kv_rows = jnp.concatenate([key_grads, value_grads], axis=1)
    gradient = jnp.dot(hidden_seq.T, kv_rows, preferred_element_type=jnp.float32)
    return attended, gradient


def reference(hidden, queries, keys, values, upstream):
    attended, gradients = lax.map(sequence_terms, (hidden, queries, keys, values, upstream))
    return attended, jnp.sum(gradients, axis=0)
```

```python
import math

import jax
import jax.numpy as jnp
from jax import lax
from jax.experimental import pallas as pl
from jax.experimental.pallas import tpu as pltpu
from jax.sharding import PartitionSpec as P

MESH = pl.DeviceIdType.MESH
HD = 128
L = 2048
ROWS = 128
B = 512
NB = L // B
G2 = 2 * HD
D = 4096
EXP_SCALE = (HD**-0.5) * math.log2(math.e)
NEG = -1e30
f32 = jnp.float32
bf16 = jnp.bfloat16

CHIPS = [(1, 2), (0, 1), (1, 1), (0, 3), (1, 3), (0, 2), (1, 0)]


def dot(a, b):
    return lax.dot_general(a, b, (((1,), (0,)), ((), ())), preferred_element_type=f32)


def col_max(s):
    return jnp.max(s.reshape(s.shape[0] // 8, 8, s.shape[1]), axis=0)


def col_sum(s):
    return jnp.sum(s.reshape(s.shape[0] // 8, 8, s.shape[1]), axis=0)


def rows_of(i, n=B):
    return pl.ds(pl.multiple_of(i * n, n), n)


def pair_index(i, j):
    return i * (i + 1) // 2 + j


def kernel(
    hid_in, q_in, k_in, v_in, g_in, att_out, grad_out,
    q_buf, g_buf, kv_buf, hid_v, ht_src, h_buf, att_buf, vt, qt_scr, s_scr, p_scr, ot_scr, li_scr,
    gt_scr, gs_scr, dd_scr, own, s1_src, s1_dst, s1_sum, s2_src, s2_dst, kv_all, acc, rs_src, rs_dst,
    q_ss, q_rs, g_ss, g_rs, kv_ss, kv_rs, sib_ss, sib_rs, h_ss, h_rs, att_ss, att_rs, hid_sem,
    s1_ss, s1_rs, s2_ss, s2_rs, s3_ss, s3_rs, s4_ss, s4_rs, rs_ss, rs_rs,
):
    dp = lax.axis_index("dp")
    me = lax.axis_index("ctx")
    xh, y, core = me // 8, (me // 2) % 4, me % 2
    sib = me + 1 - 2 * core
    group = me // 4
    half = y % 2

    def at(dx, dy, c):
        return ((xh + dx) % 2) * 8 + ((y + dy) % 4) * 2 + c

    def remote(src, dst, ss, rs, c=None, d=None):
        return pltpu.make_async_remote_copy(
            src_ref=src, dst_ref=dst, send_sem=ss, recv_sem=rs,
            device_id=(dp if d is None else d, me if c is None else c), device_id_type=MESH,
        )

    barrier = pltpu.get_barrier_semaphore()

    def greet(i, _):
        pl.semaphore_signal(barrier, inc=1, device_id=(dp, (me + i) % 16), device_id_type=MESH)
        pl.semaphore_signal(barrier, inc=1, device_id=((dp + i) % 16, me), device_id_type=MESH)
        return 0

    lax.fori_loop(1, 16, greet, 0)
    hid_copy = pltpu.make_async_copy(hid_in.at[0], hid_v, hid_sem)
    hid_copy.start()
    pl.semaphore_wait(barrier, 30)

    my_rows = rows_of(me, ROWS)

    def kv_copy(c, which):
        src = (k_in, v_in)[which].at[0, :, pl.ds(pl.multiple_of((c // 4) * HD, HD), HD)]
        return src, kv_buf.at[which, my_rows]

    def kv_send(c, which):
        src, dst = kv_copy(c, which)
        remote(src, dst, kv_ss.at[c], kv_rs.at[me], c=c).start()

    def kv_keep(which):
        src, dst = kv_copy(me, which)
        pltpu.make_async_copy(src, dst, kv_rs.at[me]).start()

    def head_cols(c):
        return pl.ds(pl.multiple_of(c * G2, G2), G2)

    def q_copy(c):
        return remote(q_in.at[0, :, head_cols(c)], q_buf.at[my_rows], q_ss.at[c], q_rs.at[me], c=c)

    def g_copy(c):
        return remote(g_in.at[0, :, head_cols(c)], g_buf.at[my_rows], g_ss.at[c], g_rs.at[me], c=c)

    def h_dst():
        return h_buf.at[:, :, my_rows]

    def h_copy(c):
        return remote(ht_src.at[:, c], h_dst(), h_ss.at[c], h_rs.at[me], c=c)

    peers = [at(dx, dy, c) for c in (0, 1) for dx, dy in CHIPS]
    for c, which in zip(peers, [0] * 7 + [1] * 7, strict=True):
        kv_send(c, which)

    @pl.when(core == 0)
    def _():
        kv_keep(0)
        kv_send(sib, 1)

    @pl.when(core == 1)
    def _():
        kv_keep(1)
        kv_send(sib, 0)

    peers = [at(dx, dy, (core + c) % 2) for c in (0, 1) for dx, dy in CHIPS] + [sib]
    for c in peers:
        q_copy(c).start()
    pltpu.make_async_copy(q_in.at[0, :, head_cols(me)], q_buf.at[my_rows], q_rs.at[me]).start()
    for c in peers:
        g_copy(c).start()
    pltpu.make_async_copy(g_in.at[0, :, head_cols(me)], g_buf.at[my_rows], g_rs.at[me]).start()

    hid_copy.wait()

    def turn(b, _):
        ht_src[b] = hid_v[:, pl.ds(pl.multiple_of(b * 256, 256), 256)].T.reshape(16, 16, ROWS)
        return 0

    lax.fori_loop(0, 16, turn, 0)
    for c in peers:
        h_copy(c).start()
    pltpu.make_async_copy(ht_src.at[:, me], h_dst(), h_rs.at[me]).start()

    def kv_wait(s, _):
        part = kv_buf.at[core, rows_of(s, ROWS)]
        pltpu.make_async_copy(part, part, kv_rs.at[s]).wait()
        return 0

    lax.fori_loop(0, 16, kv_wait, 0)
    sib_copy = remote(kv_buf.at[core], kv_buf.at[core], sib_ss, sib_rs, c=sib)
    sib_copy.start()
    theirs = kv_buf.at[1 - core]
    pltpu.make_async_copy(theirs, theirs, sib_rs).wait()

    def turn_v(j, _):
        vt[j] = kv_buf[1, rows_of(j), :].T
        return 0

    lax.fori_loop(0, NB, turn_v, 0)

    def wait_rows(buf, sems, i):
        def one(s, _):
            part = buf.at[rows_of(s, ROWS)]
            pltpu.make_async_copy(part, part, sems.at[s]).wait()
            return 0

        lax.fori_loop(4 * i, 4 * i + 4, one, 0)

    def q_turned(i):
        r = rows_of(i)
        return jnp.concatenate([q_buf[r, 0:HD].T, q_buf[r, HD:G2].T], axis=1)

    def k_block(j):
        return kv_buf[0, rows_of(j), :]

    def causal(s):
        key_at = lax.broadcasted_iota(jnp.int32, (B, 2 * B), 0)
        query_at = lax.broadcasted_iota(jnp.int32, (B, 2 * B), 1) % B
        return jnp.where(key_at <= query_at, s, NEG)

    def att_copy(s):
        return remote(
            att_buf.at[rows_of(s, ROWS)], att_out.at[0, :, head_cols(me)], att_ss.at[s], att_rs.at[me], c=s
        )

    def att_send(s, _):
        @pl.when(s != me)
        def _():
            att_copy(s).start()

        @pl.when(s == me)
        def _():
            pltpu.make_async_copy(att_buf.at[my_rows], att_out.at[0, :, head_cols(me)], att_rs.at[me]).start()

        return 0

    wait_rows(q_buf, q_rs, 0)
    first = causal(dot(k_block(0), q_turned(0)))
    s_scr[0, 0] = first

    def forward(i, top):
        now, later = i % 2, 1 - i % 2
        shift = jnp.max(top, axis=0, keepdims=True) * EXP_SCALE
        nxt = jnp.minimum(i + 1, NB - 1)

        @pl.when(i + 1 < NB)
        def _():
            wait_rows(q_buf, q_rs, i + 1)

        qt_scr[...] = q_turned(nxt)

        def weigh(j, carry):
            l, o, mn = carry
            e = jnp.exp2(s_scr[now, j] * EXP_SCALE - shift)
            l = l + col_sum(e)
            eb = e.astype(bf16)
            p_scr[pair_index(i, j)] = eb
            return l, o + dot(vt[j], eb), mn

        def step(j, carry):
            l, o, mn = carry
            s = dot(k_block(j), qt_scr[...])
            s_scr[later, j] = s
            return weigh(j, (l, o, jnp.maximum(mn, col_max(s))))

        start = (jnp.zeros((8, 2 * B), f32), jnp.zeros((HD, 2 * B), f32), jnp.full((8, 2 * B), NEG, f32))
        carry = lax.fori_loop(0, i, step, start)
        l, o, mn = lax.cond(nxt > i, lambda c: step(i, c), lambda c: weigh(i, c), carry)
        s = causal(dot(k_block(nxt), qt_scr[...]))
        s_scr[later, nxt] = s
        mn = jnp.maximum(mn, col_max(s))
        li = 1.0 / jnp.sum(l, axis=0, keepdims=True)
        o = o * li
        ot_scr[i] = o
        li_scr[i] = jnp.broadcast_to(li, (8, 2 * B))
        r = rows_of(i)
        att_buf[r, 0:HD] = o[:, 0:B].T.astype(bf16)
        att_buf[r, HD:G2] = o[:, B : 2 * B].T.astype(bf16)
        lax.fori_loop(4 * i, 4 * i + 4, att_send, 0)
        return mn

    lax.fori_loop(0, NB, forward, col_max(first))

    def prepare(i, _):
        wait_rows(g_buf, g_rs, i)
        r = rows_of(i)
        gt = jnp.concatenate([g_buf[r, 0:HD].T, g_buf[r, HD:G2].T], axis=1).astype(f32)
        gs = (gt * li_scr[i][0:1, :]).astype(bf16)
        gt_scr[i] = gs
        gs_scr[i] = gs.T
        dd = jnp.sum(gs.astype(f32) * ot_scr[i], axis=0, keepdims=True)
        dd_scr[i] = jnp.broadcast_to(dd, (8, 2 * B))
        return 0

    lax.fori_loop(0, NB, prepare, 0)

    def backward(j):
        vj = kv_buf[1, rows_of(j), :]

        def step(i, carry):
            dk, dv = carry
            eb = p_scr[pair_index(i, j)]
            dpr = dot(vj, gt_scr[i])
            ds = (eb.astype(f32) * (dpr - dd_scr[i][0:1, :])).astype(bf16)
            r = rows_of(i)
            qc = jnp.concatenate([q_buf[r, 0:HD], q_buf[r, HD:G2]], axis=0)
            return dk + dot(ds, qc), dv + dot(eb, gs_scr[i])

        zero = jnp.zeros((B, HD), f32)
        dk, dv = lax.fori_loop(j, NB, step, (zero, zero))
        dk = dk * (HD**-0.5)
        own[j, 0] = dk
        own[j, 1] = dv
        s1_src[j, 0] = dk.astype(bf16)
        s1_src[j, 1] = dv.astype(bf16)

    def s1(j):
        return remote(s1_src.at[j, 1 - core], s1_dst.at[j], s1_ss.at[j], s1_rs.at[j], c=sib)

    def s2(j):
        other = rows_of(1 - half, 256)
        return remote(
            s2_src.at[j, other], s2_dst.at[j], s2_ss.at[j], s2_rs.at[j], c=xh * 8 + (y + 1 - 2 * half) * 2 + core
        )

    def s1_done(j):
        s1(j).wait_recv()
        total = own[j, core] + s1_dst[j].astype(f32)
        s1_sum[j] = total
        s2_src[j] = total.astype(bf16)
        s2(j).start()

    def block_at(j, xh_, y_):
        rows = pl.ds(pl.multiple_of(j * B + (y_ % 2) * 256, 256), 256)
        cols = pl.ds(pl.multiple_of(core * 512 + (xh_ * 2 + y_ // 2) * HD, HD), HD)
        return rows, cols

    def s3(j, n, dx, dy):
        block = kv_all.at[block_at(j, xh, y)]
        return remote(block, block, s3_ss.at[j, n], s3_rs.at[j, xh * 4 + y], c=at(dx, dy, core))

    def s2_done(j):
        s2(j).wait_recv()
        total = s1_sum[j, rows_of(half, 256), :] + s2_dst[j].astype(f32)
        rows, cols = block_at(j, xh, y)
        kv_all[rows, cols] = total.astype(bf16)
        for n, (dx, dy) in enumerate(CHIPS):
            s3(j, n, dx, dy).start()

    def s4(j):
        part = kv_all.at[rows_of(j), pl.ds(pl.multiple_of(core * 512, 512), 512)]
        return remote(part, part, s4_ss.at[j], s4_rs.at[j], c=sib)

    def s3_done(j):
        for dx, dy in CHIPS:
            px, py = (xh + dx) % 2, (y + dy) % 4
            part = kv_all.at[block_at(j, px, py)]
            pltpu.make_async_copy(part, part, s3_rs.at[j, px * 4 + py]).wait()
        s4(j).start()

    def s4_done(j):
        part = kv_all.at[rows_of(j), pl.ds(pl.multiple_of((1 - core) * 512, 512), 512)]
        pltpu.make_async_copy(part, part, s4_rs.at[j]).wait()
        h = h_buf[:, :, j * B : (j + 1) * B].reshape(256, B)
        for n in range(4):
            cols = slice(n * 256, (n + 1) * 256)
            term = dot(h, kv_all[j * B : (j + 1) * B, cols])
            if j > 0:
                term = acc[:, cols] + term
            acc[:, cols] = term

    backward(0)
    s1(0).start()
    backward(1)
    s1(1).start()
    s1_done(0)
    backward(2)
    s1(2).start()
    s1_done(1)
    s2_done(0)
    backward(3)
    s1(3).start()
    s1_done(2)
    s2_done(1)
    s1_done(3)
    s2_done(2)
    s2_done(3)

    def h_wait(s, _):
        part = h_buf.at[:, :, rows_of(s, ROWS)]
        pltpu.make_async_copy(part, part, h_rs.at[s]).wait()
        return 0

    lax.fori_loop(0, 16, h_wait, 0)
    s3_done(0)
    s3_done(1)
    s4_done(0)
    s3_done(2)
    s4_done(1)
    s3_done(3)
    s4_done(2)
    s4_done(3)

    rs_src[...] = acc[...].astype(bf16).reshape(16, 16, 1024)

    def rs_copy(d):
        return remote(rs_src.at[d], rs_dst.at[dp], rs_ss.at[d], rs_rs.at[dp], d=d)

    def rs_send(n, _):
        rs_copy((dp + n) % 16).start()
        return 0

    lax.fori_loop(1, 16, rs_send, 0)
    grad_out[...] = acc[rows_of(dp, 16), :]

    def rs_add(n, _):
        d = (dp + 16 - n) % 16
        part = rs_dst.at[d]
        pltpu.make_async_copy(part, part, rs_rs.at[d]).wait()
        grad_out[...] += rs_dst[d].astype(f32)
        return 0

    lax.fori_loop(1, 16, rs_add, 0)

    def last(s, _):
        c = (me + s) % 16
        kv_part = kv_buf.at[0, my_rows]
        pltpu.make_async_copy(kv_part, kv_part, kv_ss.at[c]).wait()
        q_copy(c).wait_send()
        g_copy(c).wait_send()
        h_copy(c).wait_send()
        att_copy(c).wait_send()
        rs_copy((dp + s) % 16).wait_send()
        return 0

    lax.fori_loop(1, 16, last, 0)

    def att_wait(s, _):
        part = att_out.at[0, :, head_cols(s)]
        pltpu.make_async_copy(part, part, att_rs.at[s]).wait()
        return 0

    lax.fori_loop(0, 16, att_wait, 0)
    sib_copy.wait_send()
    for j in range(NB):
        s1(j).wait_send()
        s2(j).wait_send()
        for n, (dx, dy) in enumerate(CHIPS):
            s3(j, n, dx, dy).wait_send()
        s4(j).wait_send()


def per_device(hidden, queries, keys, values, upstream):
    sems = pltpu.SemaphoreType.DMA
    any_spec = pl.BlockSpec(memory_space=pl.ANY)
    pairs = NB * (NB + 1) // 2
    return pl.pallas_call(
        kernel,
        out_shape=(jax.ShapeDtypeStruct((1, ROWS, D), bf16), jax.ShapeDtypeStruct((16, 1024), f32)),
        in_specs=[any_spec] * 5,
        out_specs=(any_spec, pl.BlockSpec(memory_space=pltpu.VMEM)),
        scratch_shapes=[
            pltpu.VMEM((L, G2), bf16),
            pltpu.VMEM((L, G2), bf16),
            pltpu.VMEM((2, L, HD), bf16),
            pltpu.VMEM((ROWS, D), bf16),
            pltpu.VMEM((16, 16, 16, ROWS), bf16),
            pltpu.VMEM((16, 16, L), bf16),
            pltpu.VMEM((L, G2), bf16),
            pltpu.VMEM((NB, HD, B), bf16),
            pltpu.VMEM((HD, 2 * B), bf16),
            pltpu.VMEM((2, NB, B, 2 * B), f32),
            pltpu.VMEM((pairs, B, 2 * B), bf16),
            pltpu.VMEM((NB, HD, 2 * B), f32),
            pltpu.VMEM((NB, 8, 2 * B), f32),
            pltpu.VMEM((NB, HD, 2 * B), bf16),
            pltpu.VMEM((NB, 2 * B, HD), bf16),
            pltpu.VMEM((NB, 8, 2 * B), f32),
            pltpu.VMEM((NB, 2, B, HD), f32),
            pltpu.VMEM((NB, 2, B, HD), bf16),
            pltpu.VMEM((NB, B, HD), bf16),
            pltpu.VMEM((NB, B, HD), f32),
            pltpu.VMEM((NB, B, HD), bf16),
            pltpu.VMEM((NB, B // 2, HD), bf16),
            pltpu.VMEM((L, 1024), bf16),
            pltpu.VMEM((256, 1024), f32),
            pltpu.VMEM((16, 16, 1024), bf16),
            pltpu.VMEM((16, 16, 1024), bf16),
            sems((16,)), sems((16,)), sems((16,)), sems((16,)), sems((16,)), sems((16,)), sems, sems,
            sems((16,)), sems((16,)), sems((16,)), sems((16,)), sems,
            sems((NB,)), sems((NB,)), sems((NB,)), sems((NB,)), sems((NB, 7)), sems((NB, 8)),
            sems((NB,)), sems((NB,)), sems((16,)), sems((16,)),
        ],
        compiler_params=pltpu.CompilerParams(
            collective_id=0, has_side_effects=True, vmem_limit_bytes=56 * 2**20
        ),
        name="prefix_layer",
    )(hidden, queries, keys, values, upstream)


def solution(mesh):
    spec = P("dp", "ctx", None)
    return jax.shard_map(
        per_device,
        mesh=mesh,
        in_specs=(spec,) * 5,
        out_specs=(spec, P(("dp", "ctx"), None)),
        check_vma=False,
    )
```

```python
import math

import jax
import jax.numpy as jnp
from jax import lax
from jax.experimental import pallas as pl
from jax.experimental.pallas import tpu as pltpu
from jax.sharding import PartitionSpec as P

MESH = pl.DeviceIdType.MESH
HD = 128
L = 2048
ROWS = 128
BLK = 256
KB = 512
QC = 1024
D = 4096
EXP_SCALE = (HD**-0.5) * math.log2(math.e)
NEG = -1e30
f32 = jnp.float32
bf16 = jnp.bfloat16


def dot(a, b):
    return lax.dot_general(a, b, (((1,), (0,)), ((), ())), preferred_element_type=f32)


def col_max(s):
    return jnp.max(s.reshape(s.shape[0] // 8, 8, s.shape[1]), axis=0)


def col_sum(s):
    return jnp.sum(s.reshape(s.shape[0] // 8, 8, s.shape[1]), axis=0)


def part(i, n):
    return pl.ds(pl.multiple_of(i * n, n), n)


def kernel(
    hid_in, q_in, k_in, v_in, g_in, att_out, grad_out,
    q_buf, g_buf, kv_buf, hid_v, ht_src, h_buf, att_buf, vt, qt_scr, qs_scr, s_scr, p_scr, ot_scr, li_scr,
    gt_scr, gs_scr, dd_scr, own, y_src, y_dst, f_src, kv_all, acc, a_src, a_dst, rs_src, rs_dst,
    hid_sem, kv_ss, kv_rs, d_ss, d_rs, q_ss, q_rs, g_ss, g_rs, h_ss, h_rs, b_ss, b_rs, att_ss, att_rs,
    y_ss, y_rs, x_ss, x_rs, n_ss, n_rs, c_ss, c_rs, a_ss, a_rs, rs_ss, rs_rs,
):
    dp = lax.axis_index("dp")
    me = lax.axis_index("ctx")
    xh, y, core = me // 8, (me // 2) % 4, me % 2
    slot = xh * 2 + core
    sib = me + 1 - 2 * core
    partner = (me + 8) % 16

    def dev(x_, y_, c_):
        return x_ * 8 + y_ * 2 + c_

    def remote(src, dst, ss, rs, c=None, d=None):
        return pltpu.make_async_remote_copy(
            src_ref=src, dst_ref=dst, send_sem=ss, recv_sem=rs,
            device_id=(dp if d is None else d, me if c is None else c), device_id_type=MESH,
        )

    def local(src, dst, sem):
        return pltpu.make_async_copy(src, dst, sem)

    def arrived(ref, sem):
        pltpu.make_async_copy(ref, ref, sem).wait()

    quad = [dev(1 - xh, y, core), dev(1 - xh, y, 1 - core), sib]
    quad_slots = [(1 - xh) * 2 + core, (1 - xh) * 2 + 1 - core, xh * 2 + 1 - core]
    others = [(y + 1) % 4, (y + 3) % 4, (y + 2) % 4]
    z, xl = dp // 2, dp % 2
    x_quarters = [(1 - xh, xl), (xh, 1 - xl), (1 - xh, 1 - xl)]
    zs = [(z + n) % 8 for n in (4, 1, 7, 2, 6, 3, 5)]

    hid_copy = local(hid_in.at[0], hid_v, hid_sem)
    hid_copy.start()
    barrier = pltpu.get_barrier_semaphore()

    def greet(c=None, d=None):
        pl.semaphore_signal(
            barrier, inc=1, device_id=(dp if d is None else d, me if c is None else c), device_id_type=MESH
        )

    for c in quad[1:]:
        greet(c=c)
    for y_ in others:
        greet(c=dev(xh, y_, 0))
        greet(c=dev(xh, y_, 1))
    for x_, l_ in x_quarters:
        greet(c=dev(x_, y, core), d=z * 2 + l_)
    for z_ in zs:
        greet(d=z_ * 2 + xl)
    pl.semaphore_wait(barrier, 18)

    my_rows = part(me, ROWS)
    slot_rows = part(slot, ROWS)

    def kv_pair(s, which):
        return (k_in, v_in)[which].at[0, :, part(s, HD)], kv_buf.at[which, my_rows]

    def kv_copy(n, which):
        src, dst = kv_pair(quad_slots[n], which)
        return remote(src, dst, kv_ss.at[n, which], kv_rs.at[slot, which], c=quad[n])

    def needed(half, y_from, y_to):
        return (half == 0) | (y_to // 2 >= y_from // 2)

    def d_copy(n, c_, which):
        src, dst = kv_pair(xh * 2 + c_, which)
        return remote(src, dst, d_ss.at[n, c_, which], d_rs.at[y, core, which], c=dev(xh, others[n], c_))

    for n in range(3):
        for which in range(2):
            kv_copy(n, which).start()
    for which in range(2):
        src, dst = kv_pair(slot, which)
        local(src, dst, kv_rs.at[slot, which]).start()
    for n in range(3):

        @pl.when(needed(xh, y, others[n]))
        def _(n=n):
            for c_ in range(2):
                for which in range(2):
                    d_copy(n, c_, which).start()

    def q_copy(n):
        return remote(q_in.at[0, :, part(quad_slots[n], QC)], q_buf.at[slot_rows], q_ss.at[n], q_rs.at[slot], c=quad[n])

    def g_copy(n):
        return remote(g_in.at[0, :, part(quad_slots[n], QC)], g_buf.at[slot_rows], g_ss.at[n], g_rs.at[slot], c=quad[n])

    local(q_in.at[0, :, part(slot, QC)], q_buf.at[slot_rows], q_rs.at[slot]).start()
    local(g_in.at[0, :, part(slot, QC)], g_buf.at[slot_rows], g_rs.at[slot]).start()
    q_copy(2).start()

    hid_copy.wait()

    def turn(b, _):
        ht_src[b] = hid_v[:, part(b, 256)].T.reshape(2, 8, 16, ROWS)
        return 0

    lax.fori_loop(0, 16, turn, 0)

    for n in range(2):
        q_copy(n).start()

    def kv_wait(x_):
        for c_ in range(2):
            for which in range(2):
                arrived(kv_buf.at[which, part(dev(x_, y, c_), ROWS)], kv_rs.at[x_ * 2 + c_, which])

    def b_copy(n):
        rows = kv_buf.at[:, part((1 - xh) * 4 + y, BLK)]
        return remote(rows, rows, b_ss.at[n], b_rs.at[y], c=dev(xh, others[n], core))

    kv_wait(1 - xh)
    for n in range(3):

        @pl.when(needed(1 - xh, y, others[n]))
        def _(n=n):
            b_copy(n).start()

    kv_wait(xh)

    row_devices = [(y_, c_) for y_ in others for c_ in (core, 1 - core)] + [(y, 1 - core)]

    def h_dst():
        return h_buf.at[:, :, :, part(y * 2 + core, ROWS)]

    def h_copy(n):
        y_, c_ = row_devices[n]
        return remote(
            ht_src.at[:, :, y_ * 2 + c_], h_dst(), h_ss.at[n], h_rs.at[y * 2 + core], c=dev(xh, y_, c_)
        )

    local(ht_src.at[:, :, y * 2 + core], h_dst(), h_rs.at[y * 2 + core]).start()

    def turn_v(j):
        vt[j] = kv_buf[1, j * KB : (j + 1) * KB, :].T

    def b_wait(half):
        for y_ in others:
            wanted = needed(half, y_, y)

            @pl.when(wanted & (xh == half))
            def _(y_=y_):
                for c_ in range(2):
                    for which in range(2):
                        arrived(kv_buf.at[which, part(dev(xh, y_, c_), ROWS)], d_rs.at[y_, c_, which])

            @pl.when(wanted & (xh != half))
            def _(y_=y_):
                arrived(kv_buf.at[:, part(half * 4 + y_, BLK)], b_rs.at[y_])

        turn_v(2 * half)
        turn_v(2 * half + 1)

    halves = [xh, xh, 1 - xh, 1 - xh]
    counts = [y // 2 + 1 + 2 * h for h in halves]

    def wait_slots(buf, sems, half):
        for c_ in range(2):
            s = half * 2 + c_
            arrived(buf.at[part(s, ROWS)], sems.at[s])

    def turn_q(u):
        rows = part(halves[u], BLK)
        heads = [q_buf[rows, (u % 2) * KB + h * HD : (u % 2) * KB + (h + 1) * HD] for h in range(4)]
        qt_scr[...] = jnp.concatenate([h.T for h in heads], axis=1)
        qs_scr[halves[u] * 2 + u % 2] = jnp.concatenate(heads, axis=0)

    def k_block(j):
        return kv_buf[0, part(j, KB), :]

    def scores(u, j, mn):
        s = dot(k_block(j), qt_scr[...])
        s_scr[u % 2, j] = s
        return jnp.maximum(mn, col_max(s))

    def last_scores(u, mn):
        s = dot(k_block(counts[u] - 1), qt_scr[...])
        key_at = lax.broadcasted_iota(jnp.int32, (KB, QC), 0)
        query_at = lax.broadcasted_iota(jnp.int32, (KB, QC), 1) % BLK + (y % 2) * BLK
        s = jnp.where(key_at <= query_at, s, NEG)
        s_scr[u % 2, counts[u] - 1] = s
        return jnp.maximum(mn, col_max(s))

    def p_at(t, j):
        return jnp.where(t < 2, t * 2, t * 4 - 4) + j

    no_max = jnp.full((8, QC), NEG, f32)

    def att_copy(u, c_):
        s = halves[u] * 2 + c_
        cols = pl.ds(pl.multiple_of(slot * QC + (u % 2) * KB, KB), KB)
        src = att_buf.at[part(s, ROWS), (u % 2) * KB : (u % 2 + 1) * KB]
        return s, src, att_out.at[0, :, cols], att_rs.at[slot, u % 2]

    def att_remote(u, c_):
        s, src, dst, sem = att_copy(u, c_)
        return remote(src, dst, att_ss.at[u, c_], sem, c=dev(halves[u], y, c_))

    def forward(u, top):
        half, n = halves[u], counts[u]
        t = half * 2 + u % 2
        shift = jnp.max(top, axis=0, keepdims=True) * EXP_SCALE
        if u == 1:
            wait_slots(q_buf, q_rs, 1 - xh)

            @pl.when(xh == 0)
            def _():
                b_wait(1)

        if u < 3:
            turn_q(u + 1)

        def weigh(j, carry):
            l, o, mn = carry
            e = jnp.exp2(s_scr[u % 2, j] * EXP_SCALE - shift)
            l = l + col_sum(e)
            eb = e.astype(bf16)
            p_scr[p_at(t, j)] = eb
            return l, o + dot(vt[j], eb), mn

        def both(j, carry):
            l, o, mn = carry
            return weigh(j, (l, o, scores(u + 1, j, mn)))

        carry = (jnp.zeros((8, QC), f32), jnp.zeros((HD, QC), f32), no_max)
        if u == 3:
            l, o, mn = lax.fori_loop(0, n, weigh, carry)
        elif u == 1:
            m = counts[2] - 1
            shared = jnp.minimum(n, m)
            carry = lax.fori_loop(0, shared, both, carry)
            l, o, mn = lax.fori_loop(shared, n, weigh, carry)
            mn = lax.fori_loop(shared, m, lambda j, mx: scores(2, j, mx), mn)
            mn = last_scores(2, mn)
        else:
            carry = lax.fori_loop(0, n - 1, both, carry)
            l, o, mn = weigh(n - 1, carry)
            mn = last_scores(u + 1, mn)
        li = 1.0 / jnp.sum(l, axis=0, keepdims=True)
        o = o * li
        ot_scr[t] = o
        li_scr[t] = jnp.broadcast_to(li, (8, QC))
        rows = part(half, BLK)
        for h in range(4):
            cols = slice((u % 2) * KB + h * HD, (u % 2) * KB + (h + 1) * HD)
            att_buf[rows, cols] = o[:, h * BLK : (h + 1) * BLK].T.astype(bf16)
        for c_ in range(2):
            s, src, dst, sem = att_copy(u, c_)

            @pl.when(s == slot)
            def _(src=src, dst=dst, sem=sem):
                local(src, dst, sem).start()

            @pl.when(s != slot)
            def _(c_=c_):
                att_remote(u, c_).start()

        return mn

    wait_slots(q_buf, q_rs, xh)
    turn_q(0)
    b_wait(0)
    for n in (2, 0, 1):
        g_copy(n).start()
    for n in range(7):
        h_copy(n).start()
    early = jnp.minimum(counts[0] - 1, 2)
    top = lax.fori_loop(0, early, lambda j, mx: scores(0, j, mx), no_max)

    @pl.when(xh == 1)
    def _():
        b_wait(1)

    top = lax.fori_loop(early, counts[0] - 1, lambda j, mx: scores(0, j, mx), top)
    top = last_scores(0, top)
    for u in range(4):
        top = forward(u, top)

    for half in range(2):
        wait_slots(g_buf, g_rs, half)

    def prepare(t, _):
        rows = part(t // 2, BLK)
        heads = [g_buf[rows, pl.ds(pl.multiple_of((t % 2) * KB + h * HD, HD), HD)].T for h in range(4)]
        gt = jnp.concatenate(heads, axis=1).astype(f32)
        gs = (gt * li_scr[t][0:1, :]).astype(bf16)
        gt_scr[t] = gs
        gs_scr[t] = gs.T
        dd = jnp.sum(gs.astype(f32) * ot_scr[t], axis=0, keepdims=True)
        dd_scr[t] = jnp.broadcast_to(dd, (8, QC))
        return 0

    lax.fori_loop(0, 4, prepare, 0)

    def y_copy(half, y_to):
        return remote(
            y_src.at[half * 4 + y_to], y_dst.at[half, y], y_ss.at[half * 4 + y_to], y_rs.at[half, y],
            c=dev(xh, y_to, core),
        )

    def y_needed(half, y_from, y_to):
        return (y_from != y_to) if half == 0 else (y_from > y_to)

    def backward(j):
        vj = kv_buf[1, j * KB : (j + 1) * KB, :]
        first = (0, jnp.where(y >= 2, 0, 2), 2, jnp.where(y >= 2, 2, 4))[j]

        def step(t, carry):
            dk, dv = carry
            eb = p_scr[p_at(t, j)]
            dpr = dot(vj, gt_scr[t])
            ds = (eb.astype(f32) * (dpr - dd_scr[t][0:1, :])).astype(bf16)
            return dk + dot(ds, qs_scr[t]), dv + dot(eb, gs_scr[t])

        zero = jnp.zeros((KB, HD), f32)
        dk, dv = lax.fori_loop(first, 4, step, (zero, zero))
        dk = dk * (HD**-0.5)
        half = j // 2
        for b in range(2):
            y_to = (2 * j + b) % 4
            for which, grad in enumerate((dk, dv)):
                piece = grad[b * BLK : (b + 1) * BLK]
                own[half * 4 + y_to, which] = piece
                y_src[half * 4 + y_to, which] = piece.astype(bf16)

            @pl.when(y_needed(half, y, y_to))
            def _(half=half, y_to=y_to):
                y_copy(half, y_to).start()

    def block(p, y_, c_):
        return kv_all.at[pl.ds(c_ * 4 + p * 2, 2), part(y_, BLK)]

    def x_copy():
        return remote(f_src, block(xh, y, core), x_ss, x_rs, c=partner)

    def n_copy(p, n):
        return remote(block(p, y, core), block(p, y, core), n_ss.at[p, n], n_rs.at[p, y], c=dev(xh, others[n], core))

    def c_copy(p, y_):
        return remote(block(p, y_, core), block(p, y_, core), c_ss.at[p, y_], c_rs.at[p, y_], c=sib)

    def spread(p):
        for n in range(3):
            n_copy(p, n).start()
        c_copy(p, y).start()

    def y_sum(half):
        at = half * 4 + y
        for n in range(3):

            @pl.when(y_needed(half, others[n], y))
            def _(n=n):
                arrived(y_dst.at[half, others[n]], y_rs.at[half, others[n]])
                own[at] = own[at] + y_dst[half, others[n]].astype(f32)

        @pl.when(xh == half)
        def _():
            kv_all[pl.ds(core * 4 + xh * 2, 2), part(y, BLK)] = own[at].astype(bf16)
            spread(xh)

        @pl.when(xh != half)
        def _():
            f_src[...] = own[at].astype(bf16)
            x_copy().start()

    backward(2)
    backward(3)
    backward(0)
    y_sum(1)

    @pl.when(y < 2)
    def _():
        y_sum(0)

    backward(1)

    @pl.when(y >= 2)
    def _():
        y_sum(0)

    arrived(block(1 - xh, y, core), x_rs)
    spread(1 - xh)
    for s in range(8):
        arrived(h_buf.at[:, :, :, part(s, ROWS)], h_rs.at[s])

    def project(y_):
        for p in range(2):
            arrived(block(p, y_, 1 - core), c_rs.at[p, y_])
        h = h_buf[:, :, :, y_ * BLK : (y_ + 1) * BLK].reshape(512, BLK)
        rows = slice(y_ * BLK, (y_ + 1) * BLK)
        for n in range(4):
            kv = jnp.concatenate([kv_all[2 * n, rows, :], kv_all[2 * n + 1, rows, :]], axis=1)
            term = dot(h, kv).reshape(8, 2, 2, 16, 256)
            cols = slice(n * 256, (n + 1) * 256)
            if y_ > 0:
                term = acc[:, :, :, :, cols] + term
            acc[:, :, :, :, cols] = term

    for y_ in range(4):

        @pl.when(y != y_)
        def _(y_=y_):
            for p in range(2):
                arrived(block(p, y_, core), n_rs.at[p, y_])
                c_copy(p, y_).start()

        if y_ > 0:
            project(y_ - 1)
    project(3)

    def out_cols(b):
        c_, x_, which = b // 4, (b // 2) % 2, b % 2
        at = which * 512 + (x_ * 2 + c_) * HD
        return slice(at, at + HD)

    def a_copy(n, z_):
        x_, l_ = x_quarters[n]
        return remote(
            a_src.at[n, z_], a_dst.at[n, z_], a_ss.at[n, z_], a_rs.at[n, z_], c=dev(x_, y, core), d=z * 2 + l_
        )

    def rs_copy(z_):
        return remote(rs_src.at[z_], rs_dst.at[z], rs_ss.at[z_], rs_rs.at[z], d=z_ * 2 + xl)

    for z_ in [*zs, z]:
        for n, (x_, l_) in enumerate(x_quarters):
            for b in range(8):
                a_src[n, z_, :, out_cols(b)] = acc[z_, l_, x_, :, b * HD : (b + 1) * HD].astype(bf16)
            a_copy(n, z_).start()

    def x_total(z_, b):
        total = acc[z_, xl, xh, :, b * HD : (b + 1) * HD]
        for n in range(3):
            total = total + a_dst[n, z_, :, out_cols(b)].astype(f32)
        return total

    for z_ in zs:
        for n in range(3):
            arrived(a_dst.at[n, z_], a_rs.at[n, z_])
        for b in range(8):
            rs_src[z_, :, out_cols(b)] = x_total(z_, b).astype(bf16)
        rs_copy(z_).start()
    for n in range(3):
        arrived(a_dst.at[n, z], a_rs.at[n, z])
    for b in range(8):
        grad_out[:, out_cols(b)] = x_total(z, b)
    for z_ in zs:
        arrived(rs_dst.at[z_], rs_rs.at[z_])
        grad_out[...] += rs_dst[z_].astype(f32)

    for n in range(3):
        for which in range(2):
            kv_copy(n, which).wait_send()
        q_copy(n).wait_send()
        g_copy(n).wait_send()
        for p in range(2):
            n_copy(p, n).wait_send()

        @pl.when(needed(xh, y, others[n]))
        def _(n=n):
            for c_ in range(2):
                for which in range(2):
                    d_copy(n, c_, which).wait_send()

        @pl.when(needed(1 - xh, y, others[n]))
        def _(n=n):
            b_copy(n).wait_send()

    for n in range(7):
        h_copy(n).wait_send()
    for u in range(4):
        for c_ in range(2):

            @pl.when(halves[u] * 2 + c_ != slot)
            def _(u=u, c_=c_):
                att_remote(u, c_).wait_send()

    for s in range(4):
        for hh in range(2):
            cols = pl.ds(pl.multiple_of(s * QC + hh * KB, KB), KB)
            arrived(att_out.at[0, :, cols], att_rs.at[s, hh])
    for half in range(2):
        for y_ in range(4):

            @pl.when(y_needed(half, y, y_))
            def _(half=half, y_=y_):
                y_copy(half, y_).wait_send()

    x_copy().wait_send()
    for y_ in range(4):
        for p in range(2):
            c_copy(p, y_).wait_send()
    for z_ in range(8):
        for n in range(3):
            a_copy(n, z_).wait_send()
    for z_ in zs:
        rs_copy(z_).wait_send()


def per_device(hidden, queries, keys, values, upstream):
    sems = pltpu.SemaphoreType.DMA
    any_spec = pl.BlockSpec(memory_space=pl.ANY)
    return pl.pallas_call(
        kernel,
        out_shape=(jax.ShapeDtypeStruct((1, ROWS, D), bf16), jax.ShapeDtypeStruct((16, 1024), f32)),
        in_specs=[any_spec] * 5,
        out_specs=(any_spec, pl.BlockSpec(memory_space=pltpu.VMEM)),
        scratch_shapes=[
            pltpu.VMEM((4 * ROWS, QC), bf16),
            pltpu.VMEM((4 * ROWS, QC), bf16),
            pltpu.VMEM((2, L, HD), bf16),
            pltpu.VMEM((ROWS, D), bf16),
            pltpu.VMEM((16, 2, 8, 16, ROWS), bf16),
            pltpu.VMEM((16, 2, 16, L // 2), bf16),
            pltpu.VMEM((4 * ROWS, QC), bf16),
            pltpu.VMEM((4, HD, KB), bf16),
            pltpu.VMEM((HD, QC), bf16),
            pltpu.VMEM((4, QC, HD), bf16),
            pltpu.VMEM((2, 4, KB, QC), f32),
            pltpu.VMEM((12, KB, QC), bf16),
            pltpu.VMEM((4, HD, QC), f32),
            pltpu.VMEM((4, 8, QC), f32),
            pltpu.VMEM((4, HD, QC), bf16),
            pltpu.VMEM((4, QC, HD), bf16),
            pltpu.VMEM((4, 8, QC), f32),
            pltpu.VMEM((8, 2, BLK, HD), f32),
            pltpu.VMEM((8, 2, BLK, HD), bf16),
            pltpu.VMEM((2, 4, 2, BLK, HD), bf16),
            pltpu.VMEM((2, BLK, HD), bf16),
            pltpu.VMEM((8, L // 2, HD), bf16),
            pltpu.VMEM((8, 2, 2, 16, 1024), f32),
            pltpu.VMEM((3, 8, 16, 1024), bf16),
            pltpu.VMEM((3, 8, 16, 1024), bf16),
            pltpu.VMEM((8, 16, 1024), bf16),
            pltpu.VMEM((8, 16, 1024), bf16),
            sems, sems((3, 2)), sems((4, 2)), sems((3, 2, 2)), sems((4, 2, 2)), sems((3,)), sems((4,)), sems((3,)), sems((4,)),
            sems((7,)), sems((8,)), sems((3,)), sems((4,)), sems((4, 2)), sems((4, 2)),
            sems((8,)), sems((2, 4)), sems, sems, sems((2, 3)), sems((2, 4)), sems((2, 4)), sems((2, 4)),
            sems((3, 8)), sems((3, 8)), sems((8,)), sems((8,)),
        ],
        compiler_params=pltpu.CompilerParams(
            collective_id=0, has_side_effects=True, vmem_limit_bytes=61 * 2**20
        ),
        name="prefix_layer",
    )(hidden, queries, keys, values, upstream)


def solution(mesh):
    spec = P("dp", "ctx", None)
    return jax.shard_map(
        per_device,
        mesh=mesh,
        in_specs=(spec,) * 5,
        out_specs=(spec, P(("dp", "ctx"), None)),
        check_vma=False,
    )
```

```python
import math

import jax
import jax.numpy as jnp
from jax import lax
from jax.experimental import pallas as pl
from jax.experimental.pallas import tpu as pltpu
from jax.sharding import PartitionSpec as P

MESH = pl.DeviceIdType.MESH
HD = 128
L = 2048
ROWS = 128
BLK = 256
KB = 512
QC = 1024
D = 4096
EXP_SCALE = (HD**-0.5) * math.log2(math.e)
NEG = -1e30
f32 = jnp.float32
bf16 = jnp.bfloat16


def dot(a, b):
    return lax.dot_general(a, b, (((1,), (0,)), ((), ())), preferred_element_type=f32)


def col_max(s):
    return jnp.max(s.reshape(s.shape[0] // 8, 8, s.shape[1]), axis=0)


def col_sum(s):
    return jnp.sum(s.reshape(s.shape[0] // 8, 8, s.shape[1]), axis=0)


def part(i, n):
    return pl.ds(pl.multiple_of(i * n, n), n)


def kernel(
    hid_in, q_in, k_in, v_in, g_in, att_out, grad_out,
    q_buf, g_buf, kv_buf, hid_v, ht_src, h_buf, att_buf, vt, qt_scr, qs_scr, s_scr, p_scr, ot_scr, li_scr,
    gt_scr, gs_scr, dd_scr, own, y_src, y_dst, f_src, kv_all, acc, a_src, a_dst, rs_src, rs_dst,
    hid_sem, kv_ss, kv_rs, d_ss, d_rs, q_ss, q_rs, g_ss, g_rs, h_ss, h_rs, b_ss, b_rs, att_ss, att_rs,
    y_ss, y_rs, x_ss, x_rs, n_ss, n_rs, c_ss, c_rs, a_ss, a_rs, rs_ss, rs_rs,
):
    dp = lax.axis_index("dp")
    me = lax.axis_index("ctx")
    xh, y, core = me // 8, (me // 2) % 4, me % 2
    slot = xh * 2 + core
    sib = me + 1 - 2 * core
    partner = (me + 8) % 16

    def dev(x_, y_, c_):
        return x_ * 8 + y_ * 2 + c_

    def remote(src, dst, ss, rs, c=None, d=None):
        return pltpu.make_async_remote_copy(
            src_ref=src, dst_ref=dst, send_sem=ss, recv_sem=rs,
            device_id=(dp if d is None else d, me if c is None else c), device_id_type=MESH,
        )

    def local(src, dst, sem):
        return pltpu.make_async_copy(src, dst, sem)

    def arrived(ref, sem):
        pltpu.make_async_copy(ref, ref, sem).wait()

    quad = [dev(1 - xh, y, core), dev(1 - xh, y, 1 - core), sib]
    quad_slots = [(1 - xh) * 2 + core, (1 - xh) * 2 + 1 - core, xh * 2 + 1 - core]
    others = [(y + 1) % 4, (y + 3) % 4, (y + 2) % 4]
    z, xl = dp // 2, dp % 2
    x_quarters = [(1 - xh, xl), (xh, 1 - xl), (1 - xh, 1 - xl)]
    zs = [(z + n) % 8 for n in (4, 1, 7, 2, 6, 3, 5)]

    hid_copy = local(hid_in.at[0], hid_v, hid_sem)
    hid_copy.start()
    barrier = pltpu.get_barrier_semaphore()

    def greet(c=None, d=None):
        pl.semaphore_signal(
            barrier, inc=1, device_id=(dp if d is None else d, me if c is None else c), device_id_type=MESH
        )

    for c in quad[1:]:
        greet(c=c)
    for y_ in others:
        greet(c=dev(xh, y_, 0))
        greet(c=dev(xh, y_, 1))
    for x_, l_ in x_quarters:
        greet(c=dev(x_, y, core), d=z * 2 + l_)
    for z_ in zs:
        greet(d=z_ * 2 + xl)
    pl.semaphore_wait(barrier, 18)

    my_rows = part(me, ROWS)
    slot_rows = part(slot, ROWS)

    def kv_pair(s, which):
        return (k_in, v_in)[which].at[0, :, part(s, HD)], kv_buf.at[which, my_rows]

    def kv_copy(n, which):
        src, dst = kv_pair(quad_slots[n], which)
        return remote(src, dst, kv_ss.at[n, which], kv_rs.at[slot, which], c=quad[n])

    def needed(half, y_from, y_to):
        return (half == 0) | (y_to // 2 >= y_from // 2)

    def d_copy(n, c_, which):
        src, dst = kv_pair(xh * 2 + c_, which)
        return remote(src, dst, d_ss.at[n, c_, which], d_rs.at[y, core, which], c=dev(xh, others[n], c_))

    for n in range(3):
        for which in range(2):
            kv_copy(n, which).start()
    for which in range(2):
        src, dst = kv_pair(slot, which)
        local(src, dst, kv_rs.at[slot, which]).start()
    for n in range(3):

        @pl.when(needed(xh, y, others[n]))
        def _(n=n):
            for c_ in range(2):
                for which in range(2):
                    d_copy(n, c_, which).start()

    def q_copy(n):
        return remote(q_in.at[0, :, part(quad_slots[n], QC)], q_buf.at[slot_rows], q_ss.at[n], q_rs.at[slot], c=quad[n])

    def g_copy(n):
        return remote(g_in.at[0, :, part(quad_slots[n], QC)], g_buf.at[slot_rows], g_ss.at[n], g_rs.at[slot], c=quad[n])

    local(q_in.at[0, :, part(slot, QC)], q_buf.at[slot_rows], q_rs.at[slot]).start()
    local(g_in.at[0, :, part(slot, QC)], g_buf.at[slot_rows], g_rs.at[slot]).start()
    q_copy(2).start()

    hid_copy.wait()

    def turn(b, _):
        ht_src[b] = hid_v[:, part(b, 256)].T.reshape(2, 8, 16, ROWS)
        return 0

    lax.fori_loop(0, 16, turn, 0)

    for n in range(2):
        q_copy(n).start()

    def kv_wait(x_):
        for c_ in range(2):
            for which in range(2):
                arrived(kv_buf.at[which, part(dev(x_, y, c_), ROWS)], kv_rs.at[x_ * 2 + c_, which])

    def b_copy(n):
        rows = kv_buf.at[:, part((1 - xh) * 4 + y, BLK)]
        return remote(rows, rows, b_ss.at[n], b_rs.at[y], c=dev(xh, others[n], core))

    kv_wait(1 - xh)
    for n in range(3):

        @pl.when(needed(1 - xh, y, others[n]))
        def _(n=n):
            b_copy(n).start()

    kv_wait(xh)

    row_devices = [(y_, c_) for y_ in others for c_ in (core, 1 - core)] + [(y, 1 - core)]

    def h_dst():
        return h_buf.at[:, :, :, part(y * 2 + core, ROWS)]

    def h_copy(n):
        y_, c_ = row_devices[n]
        return remote(
            ht_src.at[:, :, y_ * 2 + c_], h_dst(), h_ss.at[n], h_rs.at[y * 2 + core], c=dev(xh, y_, c_)
        )

    local(ht_src.at[:, :, y * 2 + core], h_dst(), h_rs.at[y * 2 + core]).start()

    def turn_v(j):
        vt[j] = kv_buf[1, j * KB : (j + 1) * KB, :].T

    def b_wait(half):
        for y_ in others:
            wanted = needed(half, y_, y)

            @pl.when(wanted & (xh == half))
            def _(y_=y_):
                for c_ in range(2):
                    for which in range(2):
                        arrived(kv_buf.at[which, part(dev(xh, y_, c_), ROWS)], d_rs.at[y_, c_, which])

            @pl.when(wanted & (xh != half))
            def _(y_=y_):
                arrived(kv_buf.at[:, part(half * 4 + y_, BLK)], b_rs.at[y_])

        turn_v(2 * half)
        turn_v(2 * half + 1)

    halves = [xh, xh, 1 - xh, 1 - xh]
    counts = [y // 2 + 1 + 2 * h for h in halves]

    def wait_slots(buf, sems, half):
        for c_ in range(2):
            s = half * 2 + c_
            arrived(buf.at[part(s, ROWS)], sems.at[s])

    def turn_q(u):
        rows = part(halves[u], BLK)
        heads = [q_buf[rows, (u % 2) * KB + h * HD : (u % 2) * KB + (h + 1) * HD] for h in range(4)]
        qt_scr[...] = jnp.concatenate([h.T for h in heads], axis=1)
        qs_scr[halves[u] * 2 + u % 2] = jnp.concatenate(heads, axis=0)

    def k_block(j):
        return kv_buf[0, part(j, KB), :]

    def scores(u, j, mn):
        s = dot(k_block(j), qt_scr[...])
        s_scr[u % 2, j] = s
        return jnp.maximum(mn, col_max(s))

    def last_scores(u, mn):
        s = dot(k_block(counts[u] - 1), qt_scr[...])
        key_at = lax.broadcasted_iota(jnp.int32, (KB, QC), 0)
        query_at = lax.broadcasted_iota(jnp.int32, (KB, QC), 1) % BLK + (y % 2) * BLK
        s = jnp.where(key_at <= query_at, s, NEG)
        s_scr[u % 2, counts[u] - 1] = s
        return jnp.maximum(mn, col_max(s))

    def p_at(t, j):
        return jnp.where(t < 2, t * 2, t * 4 - 4) + j

    no_max = jnp.full((8, QC), NEG, f32)

    def att_copy(u, c_):
        s = halves[u] * 2 + c_
        cols = pl.ds(pl.multiple_of(slot * QC + (u % 2) * KB, KB), KB)
        src = att_buf.at[part(s, ROWS), (u % 2) * KB : (u % 2 + 1) * KB]
        return s, src, att_out.at[0, :, cols], att_rs.at[slot, u % 2]

    def att_remote(u, c_):
        s, src, dst, sem = att_copy(u, c_)
        return remote(src, dst, att_ss.at[u, c_], sem, c=dev(halves[u], y, c_))

    def forward(u, top):
        half, n = halves[u], counts[u]
        t = half * 2 + u % 2
        shift = jnp.max(top, axis=0, keepdims=True) * EXP_SCALE
        if u == 1:
            wait_slots(q_buf, q_rs, 1 - xh)

            @pl.when(xh == 0)
            def _():
                b_wait(1)

        if u < 3:
            turn_q(u + 1)

        def weigh(j, carry):
            l, o, mn = carry
            e = jnp.exp2(s_scr[u % 2, j] * EXP_SCALE - shift)
            l = l + col_sum(e)
            eb = e.astype(bf16)
            p_scr[p_at(t, j)] = eb
            return l, o + dot(vt[j], eb), mn

        def both(j, carry):
            l, o, mn = carry
            return weigh(j, (l, o, scores(u + 1, j, mn)))

        carry = (jnp.zeros((8, QC), f32), jnp.zeros((HD, QC), f32), no_max)
        if u == 3:
            l, o, mn = lax.fori_loop(0, n, weigh, carry)
        elif u == 1:
            m = counts[2] - 1
            shared = jnp.minimum(n, m)
            carry = lax.fori_loop(0, shared, both, carry)
            l, o, mn = lax.fori_loop(shared, n, weigh, carry)
            mn = lax.fori_loop(shared, m, lambda j, mx: scores(2, j, mx), mn)
            mn = last_scores(2, mn)
        else:
            carry = lax.fori_loop(0, n - 1, both, carry)
            l, o, mn = weigh(n - 1, carry)
            mn = last_scores(u + 1, mn)
        li = 1.0 / jnp.sum(l, axis=0, keepdims=True)
        o = o * li
        ot_scr[t] = o
        li_scr[t] = jnp.broadcast_to(li, (8, QC))
        rows = part(half, BLK)
        for h in range(4):
            cols = slice((u % 2) * KB + h * HD, (u % 2) * KB + (h + 1) * HD)
            att_buf[rows, cols] = o[:, h * BLK : (h + 1) * BLK].T.astype(bf16)
        for c_ in range(2):
            s, src, dst, sem = att_copy(u, c_)

            @pl.when(s == slot)
            def _(src=src, dst=dst, sem=sem):
                local(src, dst, sem).start()

            @pl.when(s != slot)
            def _(c_=c_):
                att_remote(u, c_).start()

        return mn

    wait_slots(q_buf, q_rs, xh)
    turn_q(0)
    b_wait(0)
    for n in (2, 0, 1):
        g_copy(n).start()
    for n in range(7):
        h_copy(n).start()
    early = jnp.minimum(counts[0] - 1, 2)
    top = lax.fori_loop(0, early, lambda j, mx: scores(0, j, mx), no_max)

    @pl.when(xh == 1)
    def _():
        b_wait(1)

    top = lax.fori_loop(early, counts[0] - 1, lambda j, mx: scores(0, j, mx), top)
    top = last_scores(0, top)
    for u in range(4):
        top = forward(u, top)

    for half in range(2):
        wait_slots(g_buf, g_rs, half)

    def prepare(t, _):
        rows = part(t // 2, BLK)
        heads = [g_buf[rows, pl.ds(pl.multiple_of((t % 2) * KB + h * HD, HD), HD)].T for h in range(4)]
        gt = jnp.concatenate(heads, axis=1).astype(f32)
        gs = (gt * li_scr[t][0:1, :]).astype(bf16)
        gt_scr[t] = gs
        gs_scr[t] = gs.T
        dd = jnp.sum(gs.astype(f32) * ot_scr[t], axis=0, keepdims=True)
        dd_scr[t] = jnp.broadcast_to(dd, (8, QC))
        return 0

    lax.fori_loop(0, 4, prepare, 0)

    def y_copy(half, y_to):
        return remote(
            y_src.at[half * 4 + y_to], y_dst.at[half, y], y_ss.at[half * 4 + y_to], y_rs.at[half, y],
            c=dev(xh, y_to, core),
        )

    def y_needed(half, y_from, y_to):
        return (y_from != y_to) if half == 0 else (y_from > y_to)

    def backward(j):
        vj = kv_buf[1, j * KB : (j + 1) * KB, :]
        first = (0, jnp.where(y >= 2, 0, 2), 2, jnp.where(y >= 2, 2, 4))[j]

        def step(t, carry):
            dk, dv = carry
            eb = p_scr[p_at(t, j)]
            dpr = dot(vj, gt_scr[t])
            ds = (eb.astype(f32) * (dpr - dd_scr[t][0:1, :])).astype(bf16)
            return dk + dot(ds, qs_scr[t]), dv + dot(eb, gs_scr[t])

        zero = jnp.zeros((KB, HD), f32)
        dk, dv = lax.fori_loop(first, 4, step, (zero, zero))
        dk = dk * (HD**-0.5)
        half = j // 2
        for b in range(2):
            y_to = (2 * j + b) % 4
            for which, grad in enumerate((dk, dv)):
                piece = grad[b * BLK : (b + 1) * BLK]
                own[half * 4 + y_to, which] = piece
                y_src[half * 4 + y_to, which] = piece.astype(bf16)

            @pl.when(y_needed(half, y, y_to))
            def _(half=half, y_to=y_to):
                y_copy(half, y_to).start()

    def block(p, y_, c_):
        return kv_all.at[pl.ds(c_ * 4 + p * 2, 2), part(y_, BLK)]

    def x_copy():
        return remote(f_src, block(xh, y, core), x_ss, x_rs, c=partner)

    def n_copy(p, n):
        return remote(block(p, y, core), block(p, y, core), n_ss.at[p, n], n_rs.at[p, y], c=dev(xh, others[n], core))

    def c_copy(p, y_):
        return remote(block(p, y_, core), block(p, y_, core), c_ss.at[p, y_], c_rs.at[p, y_], c=sib)

    def spread(p):
        for n in range(3):
            n_copy(p, n).start()
        c_copy(p, y).start()

    def y_sum(half):
        at = half * 4 + y
        for n in range(3):

            @pl.when(y_needed(half, others[n], y))
            def _(n=n):
                arrived(y_dst.at[half, others[n]], y_rs.at[half, others[n]])
                own[at] = own[at] + y_dst[half, others[n]].astype(f32)

        @pl.when(xh == half)
        def _():
            kv_all[pl.ds(core * 4 + xh * 2, 2), part(y, BLK)] = own[at].astype(bf16)
            spread(xh)

        @pl.when(xh != half)
        def _():
            f_src[...] = own[at].astype(bf16)
            x_copy().start()

    def relay():
        arrived(block(1 - xh, y, core), x_rs)
        spread(1 - xh)

    backward(0)
    backward(1)
    backward(2)
    backward(3)
    y_sum(0)
    y_sum(1)
    relay()

    for s in range(8):
        arrived(h_buf.at[:, :, :, part(s, ROWS)], h_rs.at[s])

    def project(y_):
        for p in range(2):
            arrived(block(p, y_, 1 - core), c_rs.at[p, y_])
        h = h_buf[:, :, :, y_ * BLK : (y_ + 1) * BLK].reshape(512, BLK)
        rows = slice(y_ * BLK, (y_ + 1) * BLK)
        for n in range(4):
            kv = jnp.concatenate([kv_all[2 * n, rows, :], kv_all[2 * n + 1, rows, :]], axis=1)
            term = dot(h, kv).reshape(8, 2, 2, 16, 256)
            cols = slice(n * 256, (n + 1) * 256)
            if y_ > 0:
                term = acc[:, :, :, :, cols] + term
            acc[:, :, :, :, cols] = term

    for y_ in range(4):

        @pl.when(y != y_)
        def _(y_=y_):
            for p in range(2):
                arrived(block(p, y_, core), n_rs.at[p, y_])
                c_copy(p, y_).start()

        if y_ > 0:
            project(y_ - 1)
    project(3)

    def out_cols(b):
        c_, x_, which = b // 4, (b // 2) % 2, b % 2
        at = which * 512 + (x_ * 2 + c_) * HD
        return slice(at, at + HD)

    def a_copy(n, z_):
        x_, l_ = x_quarters[n]
        return remote(
            a_src.at[n, z_], a_dst.at[n, z_], a_ss.at[n, z_], a_rs.at[n, z_], c=dev(x_, y, core), d=z * 2 + l_
        )

    def rs_copy(z_):
        return remote(rs_src.at[z_], rs_dst.at[z], rs_ss.at[z_], rs_rs.at[z], d=z_ * 2 + xl)

    for z_ in [*zs, z]:
        for n, (x_, l_) in enumerate(x_quarters):
            for b in range(8):
                a_src[n, z_, :, out_cols(b)] = acc[z_, l_, x_, :, b * HD : (b + 1) * HD].astype(bf16)
            a_copy(n, z_).start()

    def x_total(z_, b):
        total = acc[z_, xl, xh, :, b * HD : (b + 1) * HD]
        for n in range(3):
            total = total + a_dst[n, z_, :, out_cols(b)].astype(f32)
        return total

    for z_ in zs:
        for n in range(3):
            arrived(a_dst.at[n, z_], a_rs.at[n, z_])
        for b in range(8):
            rs_src[z_, :, out_cols(b)] = x_total(z_, b).astype(bf16)
        rs_copy(z_).start()
    for n in range(3):
        arrived(a_dst.at[n, z], a_rs.at[n, z])
    for b in range(8):
        grad_out[:, out_cols(b)] = x_total(z, b)
    for z_ in zs:
        arrived(rs_dst.at[z_], rs_rs.at[z_])
        grad_out[...] += rs_dst[z_].astype(f32)

    for n in range(3):
        for which in range(2):
            kv_copy(n, which).wait_send()
        q_copy(n).wait_send()
        g_copy(n).wait_send()
        for p in range(2):
            n_copy(p, n).wait_send()

        @pl.when(needed(xh, y, others[n]))
        def _(n=n):
            for c_ in range(2):
                for which in range(2):
                    d_copy(n, c_, which).wait_send()

        @pl.when(needed(1 - xh, y, others[n]))
        def _(n=n):
            b_copy(n).wait_send()

    for n in range(7):
        h_copy(n).wait_send()
    for u in range(4):
        for c_ in range(2):

            @pl.when(halves[u] * 2 + c_ != slot)
            def _(u=u, c_=c_):
                att_remote(u, c_).wait_send()

    for s in range(4):
        for hh in range(2):
            cols = pl.ds(pl.multiple_of(s * QC + hh * KB, KB), KB)
            arrived(att_out.at[0, :, cols], att_rs.at[s, hh])
    for half in range(2):
        for y_ in range(4):

            @pl.when(y_needed(half, y, y_))
            def _(half=half, y_=y_):
                y_copy(half, y_).wait_send()

    x_copy().wait_send()
    for y_ in range(4):
        for p in range(2):
            c_copy(p, y_).wait_send()
    for z_ in range(8):
        for n in range(3):
            a_copy(n, z_).wait_send()
    for z_ in zs:
        rs_copy(z_).wait_send()


def per_device(hidden, queries, keys, values, upstream):
    sems = pltpu.SemaphoreType.DMA
    any_spec = pl.BlockSpec(memory_space=pl.ANY)
    return pl.pallas_call(
        kernel,
        out_shape=(jax.ShapeDtypeStruct((1, ROWS, D), bf16), jax.ShapeDtypeStruct((16, 1024), f32)),
        in_specs=[any_spec] * 5,
        out_specs=(any_spec, pl.BlockSpec(memory_space=pltpu.VMEM)),
        scratch_shapes=[
            pltpu.VMEM((4 * ROWS, QC), bf16),
            pltpu.VMEM((4 * ROWS, QC), bf16),
            pltpu.VMEM((2, L, HD), bf16),
            pltpu.VMEM((ROWS, D), bf16),
            pltpu.VMEM((16, 2, 8, 16, ROWS), bf16),
            pltpu.VMEM((16, 2, 16, L // 2), bf16),
            pltpu.VMEM((4 * ROWS, QC), bf16),
            pltpu.VMEM((4, HD, KB), bf16),
            pltpu.VMEM((HD, QC), bf16),
            pltpu.VMEM((4, QC, HD), bf16),
            pltpu.VMEM((2, 4, KB, QC), f32),
            pltpu.VMEM((12, KB, QC), bf16),
            pltpu.VMEM((4, HD, QC), f32),
            pltpu.VMEM((4, 8, QC), f32),
            pltpu.VMEM((4, HD, QC), bf16),
            pltpu.VMEM((4, QC, HD), bf16),
            pltpu.VMEM((4, 8, QC), f32),
            pltpu.VMEM((8, 2, BLK, HD), f32),
            pltpu.VMEM((8, 2, BLK, HD), bf16),
            pltpu.VMEM((2, 4, 2, BLK, HD), bf16),
            pltpu.VMEM((2, BLK, HD), bf16),
            pltpu.VMEM((8, L // 2, HD), bf16),
            pltpu.VMEM((8, 2, 2, 16, 1024), f32),
            pltpu.VMEM((3, 8, 16, 1024), bf16),
            pltpu.VMEM((3, 8, 16, 1024), bf16),
            pltpu.VMEM((8, 16, 1024), bf16),
            pltpu.VMEM((8, 16, 1024), bf16),
            sems, sems((3, 2)), sems((4, 2)), sems((3, 2, 2)), sems((4, 2, 2)), sems((3,)), sems((4,)), sems((3,)), sems((4,)),
            sems((7,)), sems((8,)), sems((3,)), sems((4,)), sems((4, 2)), sems((4, 2)),
            sems((8,)), sems((2, 4)), sems, sems, sems((2, 3)), sems((2, 4)), sems((2, 4)), sems((2, 4)),
            sems((3, 8)), sems((3, 8)), sems((8,)), sems((8,)),
        ],
        compiler_params=pltpu.CompilerParams(
            collective_id=0, has_side_effects=True, vmem_limit_bytes=61 * 2**20
        ),
        name="prefix_layer",
    )(hidden, queries, keys, values, upstream)


def solution(mesh):
    spec = P("dp", "ctx", None)
    return jax.shard_map(
        per_device,
        mesh=mesh,
        in_specs=(spec,) * 5,
        out_specs=(spec, P(("dp", "ctx"), None)),
        check_vma=False,
    )
```

```python
import math

import jax
import jax.numpy as jnp
from jax import lax
from jax.experimental import pallas as pl
from jax.experimental.pallas import tpu as pltpu
from jax.sharding import PartitionSpec as P

MESH = pl.DeviceIdType.MESH
HD = 128
L = 2048
ROWS = 128
BLK = 256
KB = 512
QC = 1024
D = 4096
EXP_SCALE = (HD**-0.5) * math.log2(math.e)
NEG = -1e30
f32 = jnp.float32
bf16 = jnp.bfloat16


def dot(a, b):
    return lax.dot_general(a, b, (((1,), (0,)), ((), ())), preferred_element_type=f32)


def col_max(s):
    return jnp.max(s.reshape(s.shape[0] // 8, 8, s.shape[1]), axis=0)


def col_sum(s):
    return jnp.sum(s.reshape(s.shape[0] // 8, 8, s.shape[1]), axis=0)


def part(i, n):
    return pl.ds(pl.multiple_of(i * n, n), n)


def kernel(
    hid_in, q_in, k_in, v_in, g_in, att_out, grad_out,
    q_buf, g_buf, kv_buf, hid_v, ht_src, h_buf, att_buf, vt, qt_scr, qs_scr, s_scr, p_scr, ot_scr, li_scr,
    gt_scr, gs_scr, dd_scr, own, y_src, y_dst, f_src, kv_all, acc, a_src, a_dst, rs_src, rs_dst,
    hid_sem, kv_ss, kv_rs, d_ss, d_rs, q_ss, q_rs, g_ss, g_rs, h_ss, h_rs, b_ss, b_rs, att_ss, att_rs,
    y_ss, y_rs, x_ss, x_rs, n_ss, n_rs, c_ss, c_rs, a_ss, a_rs, rs_ss, rs_rs,
):
    dp = lax.axis_index("dp")
    me = lax.axis_index("ctx")
    xh, y, core = me // 8, (me // 2) % 4, me % 2
    slot = xh * 2 + core
    sib = me + 1 - 2 * core
    partner = (me + 8) % 16

    def dev(x_, y_, c_):
        return x_ * 8 + y_ * 2 + c_

    def remote(src, dst, ss, rs, c=None, d=None):
        return pltpu.make_async_remote_copy(
            src_ref=src, dst_ref=dst, send_sem=ss, recv_sem=rs,
            device_id=(dp if d is None else d, me if c is None else c), device_id_type=MESH,
        )

    def local(src, dst, sem):
        return pltpu.make_async_copy(src, dst, sem)

    def arrived(ref, sem):
        pltpu.make_async_copy(ref, ref, sem).wait()

    quad = [dev(1 - xh, y, core), dev(1 - xh, y, 1 - core), sib]
    quad_slots = [(1 - xh) * 2 + core, (1 - xh) * 2 + 1 - core, xh * 2 + 1 - core]
    others = [(y + 1) % 4, (y + 3) % 4, (y + 2) % 4]
    z, xl = dp // 2, dp % 2
    x_quarters = [(1 - xh, xl), (xh, 1 - xl), (1 - xh, 1 - xl)]
    zs = [(z + n) % 8 for n in (4, 1, 7, 2, 6, 3, 5)]

    hid_copy = local(hid_in.at[0], hid_v, hid_sem)
    hid_copy.start()
    barrier = pltpu.get_barrier_semaphore()

    def greet(c=None, d=None):
        pl.semaphore_signal(
            barrier, inc=1, device_id=(dp if d is None else d, me if c is None else c), device_id_type=MESH
        )

    for c in quad[1:]:
        greet(c=c)
    for y_ in others:
        greet(c=dev(xh, y_, 0))
        greet(c=dev(xh, y_, 1))
    for x_, l_ in x_quarters:
        greet(c=dev(x_, y, core), d=z * 2 + l_)
    for z_ in zs:
        greet(d=z_ * 2 + xl)
    pl.semaphore_wait(barrier, 18)

    my_rows = part(me, ROWS)
    slot_rows = part(slot, ROWS)

    def kv_pair(s, which):
        return (k_in, v_in)[which].at[0, :, part(s, HD)], kv_buf.at[which, my_rows]

    def kv_copy(n, which):
        src, dst = kv_pair(quad_slots[n], which)
        return remote(src, dst, kv_ss.at[n, which], kv_rs.at[slot, which], c=quad[n])

    def needed(half, y_from, y_to):
        return (half == 0) | (y_to // 2 >= y_from // 2)

    def d_copy(n, c_, which):
        src, dst = kv_pair(xh * 2 + c_, which)
        return remote(src, dst, d_ss.at[n, c_, which], d_rs.at[y, core, which], c=dev(xh, others[n], c_))

    for n in range(3):
        for which in range(2):
            kv_copy(n, which).start()
    for which in range(2):
        src, dst = kv_pair(slot, which)
        local(src, dst, kv_rs.at[slot, which]).start()
    for n in range(3):

        @pl.when(needed(xh, y, others[n]))
        def _(n=n):
            for c_ in range(2):
                for which in range(2):
                    d_copy(n, c_, which).start()

    def q_copy(n):
        return remote(q_in.at[0, :, part(quad_slots[n], QC)], q_buf.at[slot_rows], q_ss.at[n], q_rs.at[slot], c=quad[n])

    def g_copy(n):
        return remote(g_in.at[0, :, part(quad_slots[n], QC)], g_buf.at[slot_rows], g_ss.at[n], g_rs.at[slot], c=quad[n])

    local(q_in.at[0, :, part(slot, QC)], q_buf.at[slot_rows], q_rs.at[slot]).start()
    local(g_in.at[0, :, part(slot, QC)], g_buf.at[slot_rows], g_rs.at[slot]).start()
    q_copy(2).start()

    hid_copy.wait()

    def turn(b, _):
        ht_src[b] = hid_v[:, part(b, 256)].T.reshape(2, 8, 16, ROWS)
        return 0

    lax.fori_loop(0, 16, turn, 0)

    for n in range(2):
        q_copy(n).start()
    for n in (2, 0, 1):
        g_copy(n).start()

    def kv_wait(x_):
        for c_ in range(2):
            for which in range(2):
                arrived(kv_buf.at[which, part(dev(x_, y, c_), ROWS)], kv_rs.at[x_ * 2 + c_, which])

    def b_copy(n):
        rows = kv_buf.at[:, part((1 - xh) * 4 + y, BLK)]
        return remote(rows, rows, b_ss.at[n], b_rs.at[y], c=dev(xh, others[n], core))

    kv_wait(1 - xh)
    for n in range(3):

        @pl.when(needed(1 - xh, y, others[n]))
        def _(n=n):
            b_copy(n).start()

    kv_wait(xh)

    row_devices = [(y_, c_) for y_ in others for c_ in (core, 1 - core)] + [(y, 1 - core)]

    def h_dst():
        return h_buf.at[:, :, :, part(y * 2 + core, ROWS)]

    def h_copy(n):
        y_, c_ = row_devices[n]
        return remote(
            ht_src.at[:, :, y_ * 2 + c_], h_dst(), h_ss.at[n], h_rs.at[y * 2 + core], c=dev(xh, y_, c_)
        )

    local(ht_src.at[:, :, y * 2 + core], h_dst(), h_rs.at[y * 2 + core]).start()

    def turn_v(j):
        vt[j] = kv_buf[1, j * KB : (j + 1) * KB, :].T

    def b_wait(half):
        for y_ in others:
            wanted = needed(half, y_, y)

            @pl.when(wanted & (xh == half))
            def _(y_=y_):
                for c_ in range(2):
                    for which in range(2):
                        arrived(kv_buf.at[which, part(dev(xh, y_, c_), ROWS)], d_rs.at[y_, c_, which])

            @pl.when(wanted & (xh != half))
            def _(y_=y_):
                arrived(kv_buf.at[:, part(half * 4 + y_, BLK)], b_rs.at[y_])

        turn_v(2 * half)
        turn_v(2 * half + 1)

    halves = [xh, xh, 1 - xh, 1 - xh]
    counts = [y // 2 + 1 + 2 * h for h in halves]

    def wait_slots(buf, sems, half):
        for c_ in range(2):
            s = half * 2 + c_
            arrived(buf.at[part(s, ROWS)], sems.at[s])

    def turn_q(u):
        rows = part(halves[u], BLK)
        heads = [q_buf[rows, (u % 2) * KB + h * HD : (u % 2) * KB + (h + 1) * HD] for h in range(4)]
        qt_scr[...] = jnp.concatenate([h.T for h in heads], axis=1)
        qs_scr[halves[u] * 2 + u % 2] = jnp.concatenate(heads, axis=0)

    def k_block(j):
        return kv_buf[0, part(j, KB), :]

    def scores(u, j, mn):
        s = dot(k_block(j), qt_scr[...])
        s_scr[u % 2, j] = s
        return jnp.maximum(mn, col_max(s))

    def last_scores(u, mn):
        s = dot(k_block(counts[u] - 1), qt_scr[...])
        key_at = lax.broadcasted_iota(jnp.int32, (KB, QC), 0)
        query_at = lax.broadcasted_iota(jnp.int32, (KB, QC), 1) % BLK + (y % 2) * BLK
        s = jnp.where(key_at <= query_at, s, NEG)
        s_scr[u % 2, counts[u] - 1] = s
        return jnp.maximum(mn, col_max(s))

    def p_at(t, j):
        return jnp.where(t < 2, t * 2, t * 4 - 4) + j

    no_max = jnp.full((8, QC), NEG, f32)

    def att_copy(u, c_):
        s = halves[u] * 2 + c_
        cols = pl.ds(pl.multiple_of(slot * QC + (u % 2) * KB, KB), KB)
        src = att_buf.at[part(s, ROWS), (u % 2) * KB : (u % 2 + 1) * KB]
        return s, src, att_out.at[0, :, cols], att_rs.at[slot, u % 2]

    def att_remote(u, c_):
        s, src, dst, sem = att_copy(u, c_)
        return remote(src, dst, att_ss.at[u, c_], sem, c=dev(halves[u], y, c_))

    def forward(u, top):
        half, n = halves[u], counts[u]
        t = half * 2 + u % 2
        shift = jnp.max(top, axis=0, keepdims=True) * EXP_SCALE
        if u == 1:
            wait_slots(q_buf, q_rs, 1 - xh)

            @pl.when(xh == 0)
            def _():
                b_wait(1)

        if u < 3:
            turn_q(u + 1)

        def weigh(j, carry):
            l, o, mn = carry
            e = jnp.exp2(s_scr[u % 2, j] * EXP_SCALE - shift)
            l = l + col_sum(e)
            eb = e.astype(bf16)
            p_scr[p_at(t, j)] = eb
            return l, o + dot(vt[j], eb), mn

        def both(j, carry):
            l, o, mn = carry
            return weigh(j, (l, o, scores(u + 1, j, mn)))

        carry = (jnp.zeros((8, QC), f32), jnp.zeros((HD, QC), f32), no_max)
        if u == 3:
            l, o, mn = lax.fori_loop(0, n, weigh, carry)
        elif u == 1:
            m = counts[2] - 1
            shared = jnp.minimum(n, m)
            carry = lax.fori_loop(0, shared, both, carry)
            l, o, mn = lax.fori_loop(shared, n, weigh, carry)
            mn = lax.fori_loop(shared, m, lambda j, mx: scores(2, j, mx), mn)
            mn = last_scores(2, mn)
        else:
            carry = lax.fori_loop(0, n - 1, both, carry)
            l, o, mn = weigh(n - 1, carry)
            mn = last_scores(u + 1, mn)
        li = 1.0 / jnp.sum(l, axis=0, keepdims=True)
        o = o * li
        ot_scr[t] = o
        li_scr[t] = jnp.broadcast_to(li, (8, QC))
        rows = part(half, BLK)
        for h in range(4):
            cols = slice((u % 2) * KB + h * HD, (u % 2) * KB + (h + 1) * HD)
            att_buf[rows, cols] = o[:, h * BLK : (h + 1) * BLK].T.astype(bf16)
        for c_ in range(2):
            s, src, dst, sem = att_copy(u, c_)

            @pl.when(s == slot)
            def _(src=src, dst=dst, sem=sem):
                local(src, dst, sem).start()

            @pl.when(s != slot)
            def _(c_=c_):
                att_remote(u, c_).start()

        return mn

    wait_slots(q_buf, q_rs, xh)
    turn_q(0)
    b_wait(0)
    for n in range(7):
        h_copy(n).start()
    early = jnp.minimum(counts[0] - 1, 2)
    top = lax.fori_loop(0, early, lambda j, mx: scores(0, j, mx), no_max)

    @pl.when(xh == 1)
    def _():
        b_wait(1)

    top = lax.fori_loop(early, counts[0] - 1, lambda j, mx: scores(0, j, mx), top)
    top = last_scores(0, top)
    for u in range(4):
        top = forward(u, top)

    for half in range(2):
        wait_slots(g_buf, g_rs, half)

    def prepare(t, _):
        rows = part(t // 2, BLK)
        heads = [g_buf[rows, pl.ds(pl.multiple_of((t % 2) * KB + h * HD, HD), HD)].T for h in range(4)]
        gt = jnp.concatenate(heads, axis=1).astype(f32)
        gs = (gt * li_scr[t][0:1, :]).astype(bf16)
        gt_scr[t] = gs
        gs_scr[t] = gs.T
        dd = jnp.sum(gs.astype(f32) * ot_scr[t], axis=0, keepdims=True)
        dd_scr[t] = jnp.broadcast_to(dd, (8, QC))
        return 0

    lax.fori_loop(0, 4, prepare, 0)

    def y_copy(half, y_to):
        return remote(
            y_src.at[half * 4 + y_to], y_dst.at[half, y], y_ss.at[half * 4 + y_to], y_rs.at[half, y],
            c=dev(xh, y_to, core),
        )

    def y_needed(half, y_from, y_to):
        return (y_from != y_to) if half == 0 else (y_from > y_to)

    def backward(j):
        vj = kv_buf[1, j * KB : (j + 1) * KB, :]
        first = (0, jnp.where(y >= 2, 0, 2), 2, jnp.where(y >= 2, 2, 4))[j]

        def step(t, carry):
            dk, dv = carry
            eb = p_scr[p_at(t, j)]
            dpr = dot(vj, gt_scr[t])
            ds = (eb.astype(f32) * (dpr - dd_scr[t][0:1, :])).astype(bf16)
            return dk + dot(ds, qs_scr[t]), dv + dot(eb, gs_scr[t])

        zero = jnp.zeros((KB, HD), f32)
        dk, dv = lax.fori_loop(first, 4, step, (zero, zero))
        dk = dk * (HD**-0.5)
        half = j // 2
        for b in range(2):
            y_to = (2 * j + b) % 4
            for which, grad in enumerate((dk, dv)):
                piece = grad[b * BLK : (b + 1) * BLK]
                own[half * 4 + y_to, which] = piece
                y_src[half * 4 + y_to, which] = piece.astype(bf16)

            @pl.when(y_needed(half, y, y_to))
            def _(half=half, y_to=y_to):
                y_copy(half, y_to).start()

    def block(p, y_, c_):
        return kv_all.at[pl.ds(c_ * 4 + p * 2, 2), part(y_, BLK)]

    def x_copy():
        return remote(f_src, block(xh, y, core), x_ss, x_rs, c=partner)

    def n_copy(p, n):
        return remote(block(p, y, core), block(p, y, core), n_ss.at[p, n], n_rs.at[p, y], c=dev(xh, others[n], core))

    def c_copy(p, y_):
        return remote(block(p, y_, core), block(p, y_, core), c_ss.at[p, y_], c_rs.at[p, y_], c=sib)

    def spread(p):
        for n in range(3):
            n_copy(p, n).start()
        c_copy(p, y).start()

    def y_sum(half):
        at = half * 4 + y
        for n in range(3):

            @pl.when(y_needed(half, others[n], y))
            def _(n=n):
                arrived(y_dst.at[half, others[n]], y_rs.at[half, others[n]])
                own[at] = own[at] + y_dst[half, others[n]].astype(f32)

        @pl.when(xh == half)
        def _():
            kv_all[pl.ds(core * 4 + xh * 2, 2), part(y, BLK)] = own[at].astype(bf16)
            spread(xh)

        @pl.when(xh != half)
        def _():
            f_src[...] = own[at].astype(bf16)
            x_copy().start()

    def relay():
        arrived(block(1 - xh, y, core), x_rs)
        spread(1 - xh)

    backward(0)
    backward(1)
    backward(2)
    backward(3)
    y_sum(0)
    y_sum(1)
    relay()

    for s in range(8):
        arrived(h_buf.at[:, :, :, part(s, ROWS)], h_rs.at[s])

    def project(y_):
        for p in range(2):
            arrived(block(p, y_, 1 - core), c_rs.at[p, y_])
        h = h_buf[:, :, :, y_ * BLK : (y_ + 1) * BLK].reshape(512, BLK)
        rows = slice(y_ * BLK, (y_ + 1) * BLK)
        for n in range(4):
            kv = jnp.concatenate([kv_all[2 * n, rows, :], kv_all[2 * n + 1, rows, :]], axis=1)
            term = dot(h, kv).reshape(8, 2, 2, 16, 256)
            cols = slice(n * 256, (n + 1) * 256)
            if y_ > 0:
                term = acc[:, :, :, :, cols] + term
            acc[:, :, :, :, cols] = term

    for y_ in range(4):

        @pl.when(y != y_)
        def _(y_=y_):
            for p in range(2):
                arrived(block(p, y_, core), n_rs.at[p, y_])
                c_copy(p, y_).start()

        if y_ > 0:
            project(y_ - 1)
    project(3)

    def out_cols(b):
        c_, x_, which = b // 4, (b // 2) % 2, b % 2
        at = which * 512 + (x_ * 2 + c_) * HD
        return slice(at, at + HD)

    def a_copy(n, z_):
        x_, l_ = x_quarters[n]
        return remote(
            a_src.at[n, z_], a_dst.at[n, z_], a_ss.at[n, z_], a_rs.at[n, z_], c=dev(x_, y, core), d=z * 2 + l_
        )

    def rs_copy(z_):
        return remote(rs_src.at[z_], rs_dst.at[z], rs_ss.at[z_], rs_rs.at[z], d=z_ * 2 + xl)

    for z_ in [*zs, z]:
        for n, (x_, l_) in enumerate(x_quarters):
            for b in range(8):
                a_src[n, z_, :, out_cols(b)] = acc[z_, l_, x_, :, b * HD : (b + 1) * HD].astype(bf16)
            a_copy(n, z_).start()

    def x_total(z_, b):
        total = acc[z_, xl, xh, :, b * HD : (b + 1) * HD]
        for n in range(3):
            total = total + a_dst[n, z_, :, out_cols(b)].astype(f32)
        return total

    for z_ in zs:
        for n in range(3):
            arrived(a_dst.at[n, z_], a_rs.at[n, z_])
        for b in range(8):
            rs_src[z_, :, out_cols(b)] = x_total(z_, b).astype(bf16)
        rs_copy(z_).start()
    for n in range(3):
        arrived(a_dst.at[n, z], a_rs.at[n, z])
    for b in range(8):
        grad_out[:, out_cols(b)] = x_total(z, b)
    for z_ in zs:
        arrived(rs_dst.at[z_], rs_rs.at[z_])
        grad_out[...] += rs_dst[z_].astype(f32)

    for n in range(3):
        for which in range(2):
            kv_copy(n, which).wait_send()
        q_copy(n).wait_send()
        g_copy(n).wait_send()
        for p in range(2):
            n_copy(p, n).wait_send()

        @pl.when(needed(xh, y, others[n]))
        def _(n=n):
            for c_ in range(2):
                for which in range(2):
                    d_copy(n, c_, which).wait_send()

        @pl.when(needed(1 - xh, y, others[n]))
        def _(n=n):
            b_copy(n).wait_send()

    for n in range(7):
        h_copy(n).wait_send()
    for u in range(4):
        for c_ in range(2):

            @pl.when(halves[u] * 2 + c_ != slot)
            def _(u=u, c_=c_):
                att_remote(u, c_).wait_send()

    for s in range(4):
        for hh in range(2):
            cols = pl.ds(pl.multiple_of(s * QC + hh * KB, KB), KB)
            arrived(att_out.at[0, :, cols], att_rs.at[s, hh])
    for half in range(2):
        for y_ in range(4):

            @pl.when(y_needed(half, y, y_))
            def _(half=half, y_=y_):
                y_copy(half, y_).wait_send()

    x_copy().wait_send()
    for y_ in range(4):
        for p in range(2):
            c_copy(p, y_).wait_send()
    for z_ in range(8):
        for n in range(3):
            a_copy(n, z_).wait_send()
    for z_ in zs:
        rs_copy(z_).wait_send()


def per_device(hidden, queries, keys, values, upstream):
    sems = pltpu.SemaphoreType.DMA
    any_spec = pl.BlockSpec(memory_space=pl.ANY)
    return pl.pallas_call(
        kernel,
        out_shape=(jax.ShapeDtypeStruct((1, ROWS, D), bf16), jax.ShapeDtypeStruct((16, 1024), f32)),
        in_specs=[any_spec] * 5,
        out_specs=(any_spec, pl.BlockSpec(memory_space=pltpu.VMEM)),
        scratch_shapes=[
            pltpu.VMEM((4 * ROWS, QC), bf16),
            pltpu.VMEM((4 * ROWS, QC), bf16),
            pltpu.VMEM((2, L, HD), bf16),
            pltpu.VMEM((ROWS, D), bf16),
            pltpu.VMEM((16, 2, 8, 16, ROWS), bf16),
            pltpu.VMEM((16, 2, 16, L // 2), bf16),
            pltpu.VMEM((4 * ROWS, QC), bf16),
            pltpu.VMEM((4, HD, KB), bf16),
            pltpu.VMEM((HD, QC), bf16),
            pltpu.VMEM((4, QC, HD), bf16),
            pltpu.VMEM((2, 4, KB, QC), f32),
            pltpu.VMEM((12, KB, QC), bf16),
            pltpu.VMEM((4, HD, QC), f32),
            pltpu.VMEM((4, 8, QC), f32),
            pltpu.VMEM((4, HD, QC), bf16),
            pltpu.VMEM((4, QC, HD), bf16),
            pltpu.VMEM((4, 8, QC), f32),
            pltpu.VMEM((8, 2, BLK, HD), f32),
            pltpu.VMEM((8, 2, BLK, HD), bf16),
            pltpu.VMEM((2, 4, 2, BLK, HD), bf16),
            pltpu.VMEM((2, BLK, HD), bf16),
            pltpu.VMEM((8, L // 2, HD), bf16),
            pltpu.VMEM((8, 2, 2, 16, 1024), f32),
            pltpu.VMEM((3, 8, 16, 1024), bf16),
            pltpu.VMEM((3, 8, 16, 1024), bf16),
            pltpu.VMEM((8, 16, 1024), bf16),
            pltpu.VMEM((8, 16, 1024), bf16),
            sems, sems((3, 2)), sems((4, 2)), sems((3, 2, 2)), sems((4, 2, 2)), sems((3,)), sems((4,)), sems((3,)), sems((4,)),
            sems((7,)), sems((8,)), sems((3,)), sems((4,)), sems((4, 2)), sems((4, 2)),
            sems((8,)), sems((2, 4)), sems, sems, sems((2, 3)), sems((2, 4)), sems((2, 4)), sems((2, 4)),
            sems((3, 8)), sems((3, 8)), sems((8,)), sems((8,)),
        ],
        compiler_params=pltpu.CompilerParams(
            collective_id=0, has_side_effects=True, vmem_limit_bytes=61 * 2**20
        ),
        name="prefix_layer",
    )(hidden, queries, keys, values, upstream)


def solution(mesh):
    spec = P("dp", "ctx", None)
    return jax.shard_map(
        per_device,
        mesh=mesh,
        in_specs=(spec,) * 5,
        out_specs=(spec, P(("dp", "ctx"), None)),
        check_vma=False,
    )
```
